32 devices in a mesh: beam: 2 (over y), freq: 8 (over z, x), tm: 2 (over core).
Axes of the slice: x: 2, y: 2, z: 4, core: 2. Of those that a mesh axis runs over, the one named last changes fastest.
Arguments:
- intensity: float32 [128, 8192], P(('beam', 'freq'), 'tm'), parts along dimension 0, may hold values from -6 to 6
- channel_shift: int32 [64, 2], replicated, may hold values from 0 to 15, as said below
- section_shift: int32 [6, 128], replicated, may hold values from 0 to 96, as said below
- filter_bank: float32 [8, 128], replicated, may hold values from -0.5 to 0.5
Outputs:
- power_map: float32 [256, 8, 8], P(('beam', 'freq'), None, 'tm'), parts along dimension 0
The draws below stay inside these ranges and needn't reach their ends.
There are 2 independent parts, one for each index of `beam`. The reference program is written for one: setup_inputs(seed, part) draws one part's arguments, and reference() takes and returns one part's arrays. A program takes and returns all parts, laid end to end along the dimension named above; an argument that names none is the same for every part. Nothing has to cross between parts.
Inputs may be any that keep to these rules, and one draw needn't show every extreme that they name: `channel_shift`: every entry is at most 15, and some entry equals 15. `section_shift`: every entry of row s lies between 0 and 3 * 2^s, and some entry of each row s equals 3 * 2^s.
All inputs are finite; a program needn't handle non-finite values.
Results may differ from the reference program's by a relative error of at most 0.0003.
Values sent between devices are 32-bit elements; how exact they have to be, the bound alone decides.
A program may use at most 64 MiB of HBM per device.

```python
from functools import partial
import jax
import jax.numpy as jnp
from jax import lax

CHANNELS = 64
SECTIONS = 6
CH_TRIALS = 2
TRIALS = 128
TIME = 8192
SHIFT_UNIT = 3
CHAN_MAX = 15
TAPS = 128
FILTERS = 8
BLOCK = 1024


def draw_channel_shift(key, part):
    key_values, key_spot = jax.random.split(key)
    values = jax.random.randint(key_values, (CHANNELS, CH_TRIALS), 0, CHAN_MAX + 1)
    chosen_spot = jax.random.randint(key_spot, (), 0, CHANNELS * CH_TRIALS)
    positions = jnp.arange(CHANNELS * CH_TRIALS, dtype=jnp.int32).reshape(CHANNELS, CH_TRIALS)
    return jnp.where(positions == chosen_spot, CHAN_MAX, values).astype(jnp.int32)


def draw_section_shift(key, part):
    key_values, key_spot = jax.random.split(key)
    section_caps = SHIFT_UNIT * 2 ** jnp.arange(SECTIONS, dtype=jnp.int32)
    values = jax.random.randint(key_values, (SECTIONS, TRIALS), 0, 2 ** 30) % (section_caps[:, None] + 1)
    chosen_spot = jax.random.randint(key_spot, (SECTIONS, 1), 0, TRIALS)
    positions = jnp.arange(TRIALS, dtype=jnp.int32)[None, :]
    return jnp.where(positions == chosen_spot, section_caps[:, None], values).astype(jnp.int32)


def steps_of(own_key, dims, shards, least, high):
    def one(dim, parts):
        draws = jax.random.uniform(jax.random.fold_in(jax.random.fold_in(own_key, 6), dim), (parts,), jnp.float32, least / len(shards), high / len(shards))
        return jnp.repeat(jnp.exp(draws), dims[dim] // parts).reshape((-1,) + (1,) * (len(dims) - dim - 1))

    loudness = one(*shards[0])
    for cut in shards[1:]:
        loudness = loudness * one(*cut)
    return loudness


def centred(rng, extent, spread, bound, cuts=(), kind=jnp.bfloat16):
    entries = spread * jax.random.normal(rng, extent, jnp.float32)
    if cuts:
        entries = entries * steps_of(rng, extent, cuts, -0.22, 0.18)
    return jnp.clip(entries, -bound, bound).astype(kind)


def setup_inputs(seed: int = 0, part: int = 0) -> dict:
    keys = jax.random.split(jax.random.key(seed), 5)
    part_keys = jax.random.split(jax.random.fold_in(keys[4], part), 5)
    return {
        "intensity": centred(part_keys[0], (CHANNELS, TIME), 1.0, 6.0, ((0, 8), (1, 2)), jnp.float32),
        "channel_shift": draw_channel_shift(jax.random.fold_in(keys[4], 71), part),
        "section_shift": draw_section_shift(jax.random.fold_in(keys[4], 71), part),
        "filter_bank": centred(keys[3], (FILTERS, TAPS), TAPS ** -0.5, 0.5, (), jnp.float32),
    }


def take_window(one_row, amount, length):
    return lax.dynamic_slice_in_dim(one_row, amount.astype(jnp.int32), length)


def shifted_rows(row_block, shifts, length):
    return jax.vmap(partial(take_window, length=length))(row_block, shifts)


def merge_bands(lower_band, upper_ext, shift_table, out_len):
    doubled_low = jnp.concatenate([lower_band, lower_band], axis=1)[:, :, :out_len]
    doubled_up = jnp.concatenate([upper_ext, upper_ext], axis=1)
    shifted = shifted_rows(doubled_up.reshape(-1, doubled_up.shape[2]), shift_table.reshape(-1), out_len)
    return doubled_low + shifted.reshape(doubled_low.shape)


def reference(intensity, channel_shift, section_shift, filter_bank):
    channels, total_time = intensity.shape
    trials_each = channel_shift.shape[1]
    padded = jnp.concatenate([intensity, jnp.zeros((channels, CHAN_MAX), intensity.dtype)], axis=1)
    tree_rows = shifted_rows(jnp.repeat(padded, trials_each, axis=0), channel_shift.reshape(-1), total_time)
    tree_rows = tree_rows.reshape(channels, trials_each, total_time)
    for section_index in range(SECTIONS):
        max_shift = SHIFT_UNIT * 2 ** section_index
        band_count, band_rows, span_len = tree_rows.shape
        lower_band = tree_rows[0::2]
        upper_band = tree_rows[1::2]
        upper_ext = jnp.concatenate([upper_band, jnp.zeros((band_count // 2, band_rows, max_shift), tree_rows.dtype)], axis=2)
        shift_table = section_shift[section_index].reshape(band_count // 2, 2 * band_rows)
        tree_rows = merge_bands(lower_band, upper_ext, shift_table, total_time)
    dedispersed = tree_rows.reshape(-1, total_time)
    row_count = dedispersed.shape[0]
    fft_size = 2 * total_time
    spectrum = jnp.fft.rfft(dedispersed, n=fft_size, axis=1)

    def one_filter(kernel):
        kernel_spec = jnp.fft.rfft(kernel, n=fft_size)
        series = jnp.fft.irfft(spectrum * jnp.conj(kernel_spec)[None, :], n=fft_size, axis=1)[:, :total_time]
        return jnp.sum((series * series).reshape(row_count, total_time // BLOCK, BLOCK), axis=2)

    power_map = lax.map(one_filter, filter_bank)
    return jnp.transpose(power_map, (1, 0, 2)) / (BLOCK * CHANNELS)
```

```python
import functools

import jax
import jax.numpy as jnp
from jax import lax
from jax.experimental import pallas as pl
from jax.experimental.pallas import tpu as pltpu
from jax.sharding import PartitionSpec as P

SHIFT_UNIT = 3
CHAN_MAX = 15
BLOCK = 1024


def from_behind(block, axis, distance):
    devices = range(lax.axis_size(axis))
    route = [(i - distance, i) for i in devices if i - distance in devices]
    return lax.ppermute(block, axis, route)


def from_partner(array, axis, distance):
    return lax.ppermute(array, axis, [(i, i ^ 1 << distance) for i in range(lax.axis_size(axis))])


def shifted_rows(row_block, shifts, length):
    extra = row_block.shape[1] - length
    bit_count = max(extra, 0).bit_length()
    target = length + 2**bit_count - 1
    current = row_block
    if target > row_block.shape[1]:
        current = jnp.concatenate(
            [
                row_block,
                jnp.zeros((row_block.shape[0], target - row_block.shape[1]), row_block.dtype),
            ],
            axis=1,
        )
    for bit_index in range(bit_count - 1, -1, -1):
        step = 2**bit_index
        chosen = jnp.bitwise_and(jnp.right_shift(shifts, bit_index), 1)[:, None] == 1
        current = jnp.where(chosen, current[:, step:], current[:, : current.shape[1] - step])
    return current


def merge_bands(lower_band, upper_ext, shift_table, out_len):
    doubled_low = jnp.concatenate([lower_band, lower_band], axis=1)[:, :, :out_len]
    doubled_up = jnp.concatenate([upper_ext, upper_ext], axis=1)
    shifted = shifted_rows(
        doubled_up.reshape(-1, doubled_up.shape[2]), shift_table.reshape(-1), out_len
    )
    return doubled_low + shifted.reshape(doubled_low.shape)


def toeplitz_pair(filter_bank):
    tap_count = filter_bank.shape[1]
    lag_index = jnp.arange(tap_count)[:, None] - jnp.arange(tap_count)[None, :]
    toep_top = jnp.where(
        lag_index >= 0, jnp.take(filter_bank, jnp.clip(lag_index, 0, tap_count - 1), axis=1), 0.0
    )
    lag_later = lag_index + tap_count
    toep_low = jnp.where(
        lag_later < tap_count,
        jnp.take(filter_bank, jnp.clip(lag_later, 0, tap_count - 1), axis=1),
        0.0,
    )
    return (toep_top, toep_low)


def body(intensity, channel_shift, section_shift, filter_bank):
    chan_dev, samples = intensity.shape
    n_freq = lax.axis_size("freq")
    local_levels = chan_dev.bit_length() - 1
    freq_levels = n_freq.bit_length() - 1
    trials_each = channel_shift.shape[1]
    row_count = trials_each * chan_dev
    channels = chan_dev * n_freq
    freq_place = lax.axis_index("freq")
    own_section = lax.dynamic_slice_in_dim(section_shift, freq_place * row_count, row_count, 1)
    local_margin = SHIFT_UNIT * (2**local_levels - 1)
    margin = CHAN_MAX + local_margin
    rim_cols = from_behind(intensity[:, :margin], "tm", -1)
    extended = jnp.concatenate([intensity, rim_cols], axis=1)
    own_chan_shift = lax.dynamic_slice_in_dim(channel_shift, freq_place * chan_dev, chan_dev, 0)
    length = samples + margin - CHAN_MAX
    tree_rows = shifted_rows(
        jnp.repeat(extended, trials_each, axis=0), own_chan_shift.reshape(-1), length
    )
    tree_rows = tree_rows.reshape(chan_dev, trials_each, length)
    for section_index in range(local_levels):
        max_shift = SHIFT_UNIT * 2**section_index
        band_count, band_rows, span_len = tree_rows.shape
        lower_band = tree_rows[0::2]
        upper_band = tree_rows[1::2]
        out_len = span_len - max_shift
        upper_ext = upper_band
        shift_table = own_section[section_index].reshape(band_count // 2, 2 * band_rows)
        tree_rows = merge_bands(lower_band, upper_ext, shift_table, out_len)
    own_rows = tree_rows.reshape(row_count, samples)
    first_cross = 0
    for section_index in range(first_cross, freq_levels):
        max_shift = SHIFT_UNIT * 2 ** (local_levels + section_index)
        shift_table = own_section[local_levels + section_index]
        upper_bit = jnp.bitwise_and(jnp.right_shift(freq_place, section_index), 1)
        is_upper = upper_bit == 1
        sent_rows = own_rows
        partner_rows = from_partner(sent_rows, "freq", section_index)
        lower_band = jnp.where(is_upper, partner_rows, sent_rows)
        upper_band = jnp.where(is_upper, sent_rows, partner_rows)
        upper_rim = from_behind(upper_band[:, :max_shift], "tm", -1)
        upper_ext = jnp.concatenate([upper_band, upper_rim], axis=1)
        own_rows = lower_band + shifted_rows(upper_ext, shift_table, samples)
    tap_count = filter_bank.shape[1]
    filters = filter_bank.shape[0]
    tail_rows = from_behind(own_rows[:, : tap_count - 1], "tm", -1)
    padded = jnp.concatenate(
        [own_rows, tail_rows, jnp.zeros((row_count, 1), own_rows.dtype)], axis=1
    )
    first_half = padded[:, :samples].reshape(-1, tap_count)
    second_half = padded[:, tap_count:].reshape(-1, tap_count)
    toep_top, toep_low = toeplitz_pair(filter_bank)
    outputs = []
    for filter_index in range(filters):
        series = jnp.dot(
            first_half,
            toep_top[filter_index],
            precision=lax.Precision.HIGHEST,
            preferred_element_type=jnp.float32,
        )
        series = series + jnp.dot(
            second_half,
            toep_low[filter_index],
            precision=lax.Precision.HIGHEST,
            preferred_element_type=jnp.float32,
        )
        energy = jnp.sum((series * series).reshape(row_count, samples // BLOCK, BLOCK), axis=2)
        outputs.append(energy)
    return jnp.stack(outputs, axis=1) / (BLOCK * channels)


LANES = 128
GROUP = 8
TILES = 8
MESH = pl.DeviceIdType.MESH


def butterfly_partner(place, mask):
    partner = place
    for bit in range(3):
        if mask >> bit & 1:
            own = (place // 2**bit) % 2
            partner = partner + (1 - 2 * own) * 2**bit
    return partner


def advanced(row, following, amount, lane):
    picked = jnp.where(lane < amount, following, row)
    return pltpu.roll(picked, (LANES - amount) % LANES, 1)


def next_sublane(row):
    return pltpu.roll(row, TILES - 1, 0)


def butterflies(rows, shift_of, lane):
    for section in range(3):
        gap = 2**section
        merged = list(rows)
        for low in range(8):
            if low & gap:
                continue
            up = rows[low + gap]
            following = next_sublane(up)
            merged[low] = rows[low] + advanced(up, following, shift_of(section, low), lane)
            merged[low + gap] = rows[low] + advanced(
                up, following, shift_of(section, low + gap), lane
            )
        rows = merged
    return rows


def split(values):
    high = values.astype(jnp.bfloat16)
    low = (values - high.astype(jnp.float32)).astype(jnp.bfloat16)
    return high, low


def kernel(
    own_tiles,
    window,
    chan_shift,
    sec_shift,
    bank,
    samples_in,
    out,
    arrived,
    series,
    weight_high,
    weight_low,
    energies,
    local_sem,
    send_sem,
    recv_sem,
    rim_send_sem,
    rim_recv_sem,
    out_send_sem,
    out_recv_sem,
):
    me = lax.axis_index("freq")
    half = lax.axis_index("tm")
    last = GROUP - 1
    own_rows = own_tiles * 8
    window_rows = window * 8
    rim_rows = window_rows - own_rows
    is_last = me == last
    lane = lax.broadcasted_iota(jnp.int32, (TILES, LANES), 1)

    barrier = pltpu.get_barrier_semaphore()
    for mask in range(1, GROUP):
        pl.semaphore_signal(
            barrier, inc=1, device_id={"freq": butterfly_partner(me, mask)}, device_id_type=MESH
        )

    @pl.when(jnp.logical_and(is_last, half == 0))
    def _():
        for place in range(GROUP):
            pl.semaphore_signal(
                barrier, inc=1, device_id={"freq": place, "tm": 1}, device_id_type=MESH
            )

    def own_copy(rows):
        return pltpu.make_async_copy(
            samples_in.at[pl.ds(me * own_rows, rows), :],
            arrived.at[me, pl.ds(0, rows), :],
            local_sem,
        )

    def sent(target, rows):
        return pltpu.make_async_remote_copy(
            src_ref=samples_in.at[pl.ds(target * own_rows, rows), :],
            dst_ref=arrived.at[me, pl.ds(0, rows), :],
            send_sem=send_sem.at[target],
            recv_sem=recv_sem.at[me],
            device_id={"freq": target},
            device_id_type=MESH,
        )

    def awaited(source, rows):
        return pltpu.make_async_remote_copy(
            src_ref=samples_in.at[pl.ds(0, rows), :],
            dst_ref=arrived.at[source, pl.ds(0, rows), :],
            send_sem=send_sem.at[source],
            recv_sem=recv_sem.at[source],
            device_id={"freq": source},
            device_id_type=MESH,
        )

    def rim():
        return pltpu.make_async_remote_copy(
            src_ref=samples_in.at[pl.ds(0, rim_rows), :],
            dst_ref=arrived.at[me, pl.ds(own_rows, rim_rows), :],
            send_sem=rim_send_sem,
            recv_sem=rim_recv_sem.at[me],
            device_id={"freq": last, "tm": 0},
            device_id_type=MESH,
        )

    def rim_awaited(source):
        return pltpu.make_async_remote_copy(
            src_ref=samples_in.at[pl.ds(0, rim_rows), :],
            dst_ref=arrived.at[source, pl.ds(own_rows, rim_rows), :],
            send_sem=rim_send_sem,
            recv_sem=rim_recv_sem.at[source],
            device_id={"freq": last, "tm": 1},
            device_id_type=MESH,
        )

    @pl.when(is_last)
    def _():
        own_copy(own_rows).start()

    @pl.when(jnp.logical_not(is_last))
    def _():
        own_copy(window_rows).start()

    for source in range(GROUP):
        arrived[source, window_rows:, :] = jnp.zeros((TILES * 8 - window_rows, LANES), jnp.float32)

    @pl.when(jnp.logical_and(is_last, half == 1))
    def _():
        for source in range(GROUP):
            arrived[source, own_rows:window_rows, :] = jnp.zeros((rim_rows, LANES), jnp.float32)

    pl.semaphore_wait(barrier, GROUP - 1 + half)

    for mask in (6, 7, 4, 5, 2, 3, 1):
        target = butterfly_partner(me, mask)

        @pl.when(target == last)
        def _():
            sent(target, own_rows).start()

        @pl.when(target != last)
        def _():
            sent(target, window_rows).start()

    @pl.when(half == 1)
    def _():
        rim().start()

    padded = jnp.concatenate([bank[...], jnp.zeros_like(bank[...])], axis=1)
    filters = padded.shape[0]
    for index in range(filters):
        spread = jnp.broadcast_to(padded[index : index + 1], (LANES, 2 * LANES))
        band = pltpu.roll(spread, 0, 1, stride=1, stride_axis=0)
        high, low = split(band)
        weight_high[pl.ds(index * LANES, LANES), :] = high
        weight_low[pl.ds(index * LANES, LANES), :] = low

    def take_source(source):
        @pl.loop(0, 2)
        def _(trial):
            rows = []
            for channel in range(8):
                raw = arrived[source, pl.ds(channel, TILES, stride=8), :]
                amount = chan_shift[trial, source * 8 + channel]
                rows.append(advanced(raw, next_sublane(raw), amount, lane))
            rows = butterflies(
                rows, lambda s, p: sec_shift[s, source * 16 + p * 2 + trial], lane
            )
            for position in range(8):
                start = pl.multiple_of((source * 16 + position * 2 + trial) * TILES, TILES)
                series[pl.ds(start, TILES), :] = rows[position]

    @pl.when(is_last)
    def _():
        own_copy(own_rows).wait()

    @pl.when(jnp.logical_not(is_last))
    def _():
        own_copy(window_rows).wait()

    for mask in (0, 1, 2, 3, 4, 5, 6, 7):
        source = butterfly_partner(me, mask)
        if mask:

            @pl.when(is_last)
            def _():
                awaited(source, own_rows).wait_recv()

            @pl.when(jnp.logical_not(is_last))
            def _():
                awaited(source, window_rows).wait_recv()

        @pl.when(jnp.logical_and(is_last, half == 0))
        def _():
            rim_awaited(source).wait_recv()

        take_source(source)

    @pl.loop(0, 16)
    def _(row):
        places = [pl.multiple_of((row + 16 * p) * TILES, TILES) for p in range(8)]
        rows = [series[pl.ds(place, TILES), :] for place in places]
        rows = butterflies(rows, lambda s, p: sec_shift[s + 3, row + 16 * p], lane)
        for place, values in zip(places, rows):
            series[pl.ds(place, TILES), :] = values

    tiles = [split(series[pl.ds(tile, LANES, stride=TILES), :]) for tile in range(own_tiles + 1)]
    inputs = [
        jnp.concatenate(
            [
                jnp.concatenate([tiles[tile][part], tiles[tile + 1][part]], axis=1)
                for tile in range(own_tiles)
            ],
            axis=0,
        )
        for part in range(2)
    ]

    def product(left, right):
        return lax.dot_general(
            left, right, (((1,), (1,)), ((), ())), preferred_element_type=jnp.float32
        )

    sums = []
    for index in range(filters):
        high = weight_high[pl.ds(index * LANES, LANES), :]
        low = weight_low[pl.ds(index * LANES, LANES), :]
        filtered = product(high, inputs[0]) + product(high, inputs[1]) + product(low, inputs[0])
        energy = jnp.sum(filtered * filtered, axis=0, keepdims=True)
        total = energy[:, :LANES]
        for tile in range(1, own_tiles):
            total = total + energy[:, tile * LANES : (tile + 1) * LANES]
        sums.append(total)
    energies[me] = jnp.concatenate(sums, axis=0)

    def energy_copy(target, place):
        return pltpu.make_async_remote_copy(
            src_ref=energies.at[me],
            dst_ref=energies.at[place],
            send_sem=out_send_sem.at[target],
            recv_sem=out_recv_sem.at[place],
            device_id={"freq": target},
            device_id_type=MESH,
        )

    for mask in (6, 7, 4, 5, 2, 3, 1):
        energy_copy(butterfly_partner(me, mask), me).start()
    for mask in (1, 2, 3, 4, 5, 6, 7):
        partner = butterfly_partner(me, mask)
        energy_copy(partner, partner).wait_recv()
    turn = ((GROUP - me) % GROUP) * 16
    per_block = GROUP // out.shape[1]
    for block in range(out.shape[1]):
        total = energies[block * per_block]
        for place in range(block * per_block + 1, (block + 1) * per_block):
            total = total + energies[place]
        total = pltpu.roll(total, turn, 1) * (1.0 / (BLOCK * GROUP * 8))
        for index in range(filters):
            out[index, block : block + 1, :] = total[index : index + 1, : out.shape[2]]

    for mask in range(1, GROUP):
        target = butterfly_partner(me, mask)

        @pl.when(target == last)
        def _():
            sent(target, own_rows).wait_send()

        @pl.when(target != last)
        def _():
            sent(target, window_rows).wait_send()

        energy_copy(target, me).wait_send()

    @pl.when(half == 1)
    def _():
        rim().wait_send()


def fused_body(intensity, channel_shift, section_shift, filter_bank):
    chan_dev, samples = intensity.shape
    tile_count = samples // LANES
    own_tiles = tile_count // GROUP
    reach = CHAN_MAX + SHIFT_UNIT * (2 ** section_shift.shape[0] - 1) + LANES
    window = own_tiles + -(-reach // LANES)
    filters = filter_bank.shape[0]
    blocks = samples // BLOCK
    by_tile = intensity.reshape(chan_dev, tile_count, LANES).transpose(1, 0, 2)
    by_tile = by_tile.reshape(tile_count * chan_dev, LANES)
    smem = pl.BlockSpec(memory_space=pltpu.SMEM)
    vmem = pl.BlockSpec(memory_space=pltpu.VMEM)
    dma = pltpu.SemaphoreType.DMA
    maps = pl.pallas_call(
        functools.partial(kernel, own_tiles, window),
        out_shape=jax.ShapeDtypeStruct((filters, blocks, LANES // GROUP), jnp.float32),
        in_specs=[smem, smem, vmem, pl.BlockSpec(memory_space=pl.ANY)],
        out_specs=vmem,
        scratch_shapes=[
            pltpu.VMEM((GROUP, TILES * chan_dev, LANES), jnp.float32),
            pltpu.VMEM((LANES * TILES, LANES), jnp.float32),
            pltpu.VMEM((filters * LANES, 2 * LANES), jnp.bfloat16),
            pltpu.VMEM((filters * LANES, 2 * LANES), jnp.bfloat16),
            pltpu.VMEM((GROUP, filters, LANES), jnp.float32),
            dma,
            dma((GROUP,)),
            dma((GROUP,)),
            dma,
            dma((GROUP,)),
            dma((GROUP,)),
            dma((GROUP,)),
        ],
        compiler_params=pltpu.CompilerParams(
            collective_id=0, has_side_effects=True, vmem_limit_bytes=32 * 2**20
        ),
    )(channel_shift.T, section_shift, filter_bank, by_tile)
    return maps.transpose(2, 0, 1)


def fits_fused(mesh, intensity, channel_shift, section_shift, filter_bank):
    groups, halves = mesh.shape["freq"], mesh.shape["tm"]
    samples = intensity.shape[1] // halves
    channels, trials_each = channel_shift.shape
    own = samples // groups
    reach = CHAN_MAX + SHIFT_UNIT * (2 ** section_shift.shape[0] - 1) + LANES
    return (
        groups == GROUP
        and halves == 2
        and channels == 8 * GROUP
        and trials_each == 2
        and filter_bank.shape == (8, LANES)
        and own % LANES == 0
        and BLOCK % own == 0
        and reach <= own
        and own + reach <= (TILES - 1) * LANES
    )


def solution(mesh):
    in_specs = (P(("beam", "freq"), "tm"), P(), P(), P())
    out_specs = P(("beam", "freq"), None, "tm")

    def whole(*arrays):
        chosen = fused_body if fits_fused(mesh, *arrays) else body
        return jax.shard_map(
            chosen, mesh=mesh, in_specs=in_specs, out_specs=out_specs, check_vma=False
        )(*arrays)

    return whole
```

```python
import functools

import jax
import jax.numpy as jnp
from jax import lax
from jax.experimental import pallas as pl
from jax.experimental.pallas import tpu as pltpu
from jax.sharding import PartitionSpec as P

SHIFT_UNIT = 3
CHAN_MAX = 15
BLOCK = 1024


def from_behind(block, axis, distance):
    devices = range(lax.axis_size(axis))
    route = [(i - distance, i) for i in devices if i - distance in devices]
    return lax.ppermute(block, axis, route)


def from_partner(array, axis, distance):
    return lax.ppermute(array, axis, [(i, i ^ 1 << distance) for i in range(lax.axis_size(axis))])


def shifted_rows(row_block, shifts, length):
    extra = row_block.shape[1] - length
    bit_count = max(extra, 0).bit_length()
    target = length + 2**bit_count - 1
    current = row_block
    if target > row_block.shape[1]:
        current = jnp.concatenate(
            [
                row_block,
                jnp.zeros((row_block.shape[0], target - row_block.shape[1]), row_block.dtype),
            ],
            axis=1,
        )
    for bit_index in range(bit_count - 1, -1, -1):
        step = 2**bit_index
        chosen = jnp.bitwise_and(jnp.right_shift(shifts, bit_index), 1)[:, None] == 1
        current = jnp.where(chosen, current[:, step:], current[:, : current.shape[1] - step])
    return current


def merge_bands(lower_band, upper_ext, shift_table, out_len):
    doubled_low = jnp.concatenate([lower_band, lower_band], axis=1)[:, :, :out_len]
    doubled_up = jnp.concatenate([upper_ext, upper_ext], axis=1)
    shifted = shifted_rows(
        doubled_up.reshape(-1, doubled_up.shape[2]), shift_table.reshape(-1), out_len
    )
    return doubled_low + shifted.reshape(doubled_low.shape)


def toeplitz_pair(filter_bank):
    tap_count = filter_bank.shape[1]
    lag_index = jnp.arange(tap_count)[:, None] - jnp.arange(tap_count)[None, :]
    toep_top = jnp.where(
        lag_index >= 0, jnp.take(filter_bank, jnp.clip(lag_index, 0, tap_count - 1), axis=1), 0.0
    )
    lag_later = lag_index + tap_count
    toep_low = jnp.where(
        lag_later < tap_count,
        jnp.take(filter_bank, jnp.clip(lag_later, 0, tap_count - 1), axis=1),
        0.0,
    )
    return (toep_top, toep_low)


def body(intensity, channel_shift, section_shift, filter_bank):
    chan_dev, samples = intensity.shape
    n_freq = lax.axis_size("freq")
    local_levels = chan_dev.bit_length() - 1
    freq_levels = n_freq.bit_length() - 1
    trials_each = channel_shift.shape[1]
    row_count = trials_each * chan_dev
    channels = chan_dev * n_freq
    freq_place = lax.axis_index("freq")
    own_section = lax.dynamic_slice_in_dim(section_shift, freq_place * row_count, row_count, 1)
    local_margin = SHIFT_UNIT * (2**local_levels - 1)
    margin = CHAN_MAX + local_margin
    rim_cols = from_behind(intensity[:, :margin], "tm", -1)
    extended = jnp.concatenate([intensity, rim_cols], axis=1)
    own_chan_shift = lax.dynamic_slice_in_dim(channel_shift, freq_place * chan_dev, chan_dev, 0)
    length = samples + margin - CHAN_MAX
    tree_rows = shifted_rows(
        jnp.repeat(extended, trials_each, axis=0), own_chan_shift.reshape(-1), length
    )
    tree_rows = tree_rows.reshape(chan_dev, trials_each, length)
    for section_index in range(local_levels):
        max_shift = SHIFT_UNIT * 2**section_index
        band_count, band_rows, span_len = tree_rows.shape
        lower_band = tree_rows[0::2]
        upper_band = tree_rows[1::2]
        out_len = span_len - max_shift
        upper_ext = upper_band
        shift_table = own_section[section_index].reshape(band_count // 2, 2 * band_rows)
        tree_rows = merge_bands(lower_band, upper_ext, shift_table, out_len)
    own_rows = tree_rows.reshape(row_count, samples)
    first_cross = 0
    for section_index in range(first_cross, freq_levels):
        max_shift = SHIFT_UNIT * 2 ** (local_levels + section_index)
        shift_table = own_section[local_levels + section_index]
        upper_bit = jnp.bitwise_and(jnp.right_shift(freq_place, section_index), 1)
        is_upper = upper_bit == 1
        sent_rows = own_rows
        partner_rows = from_partner(sent_rows, "freq", section_index)
        lower_band = jnp.where(is_upper, partner_rows, sent_rows)
        upper_band = jnp.where(is_upper, sent_rows, partner_rows)
        upper_rim = from_behind(upper_band[:, :max_shift], "tm", -1)
        upper_ext = jnp.concatenate([upper_band, upper_rim], axis=1)
        own_rows = lower_band + shifted_rows(upper_ext, shift_table, samples)
    tap_count = filter_bank.shape[1]
    filters = filter_bank.shape[0]
    tail_rows = from_behind(own_rows[:, : tap_count - 1], "tm", -1)
    padded = jnp.concatenate(
        [own_rows, tail_rows, jnp.zeros((row_count, 1), own_rows.dtype)], axis=1
    )
    first_half = padded[:, :samples].reshape(-1, tap_count)
    second_half = padded[:, tap_count:].reshape(-1, tap_count)
    toep_top, toep_low = toeplitz_pair(filter_bank)
    outputs = []
    for filter_index in range(filters):
        series = jnp.dot(
            first_half,
            toep_top[filter_index],
            precision=lax.Precision.HIGHEST,
            preferred_element_type=jnp.float32,
        )
        series = series + jnp.dot(
            second_half,
            toep_low[filter_index],
            precision=lax.Precision.HIGHEST,
            preferred_element_type=jnp.float32,
        )
        energy = jnp.sum((series * series).reshape(row_count, samples // BLOCK, BLOCK), axis=2)
        outputs.append(energy)
    return jnp.stack(outputs, axis=1) / (BLOCK * channels)


LANES = 128
GROUP = 8
TILES = 8
MESH = pl.DeviceIdType.MESH


def butterfly_partner(place, mask):
    partner = place
    for bit in range(3):
        if mask >> bit & 1:
            own = (place // 2**bit) % 2
            partner = partner + (1 - 2 * own) * 2**bit
    return partner


def advanced(row, following, amount, lane):
    picked = jnp.where(lane < amount, following, row)
    return pltpu.roll(picked, (LANES - amount) % LANES, 1)


def next_sublane(row):
    return pltpu.roll(row, TILES - 1, 0)


def butterflies(rows, shift_of, lane):
    for section in range(3):
        gap = 2**section
        merged = list(rows)
        for low in range(8):
            if low & gap:
                continue
            up = rows[low + gap]
            following = next_sublane(up)
            merged[low] = rows[low] + advanced(up, following, shift_of(section, low), lane)
            merged[low + gap] = rows[low] + advanced(
                up, following, shift_of(section, low + gap), lane
            )
        rows = merged
    return rows


def split(values):
    high = values.astype(jnp.bfloat16)
    low = (values - high.astype(jnp.float32)).astype(jnp.bfloat16)
    return high, low


def kernel(
    own_tiles,
    window,
    chan_shift_in,
    sec_shift_in,
    bank_in,
    samples_in,
    out,
    chan_shift,
    sec_shift,
    bank,
    arrived,
    series,
    weights,
    energies,
    table_sem,
    local_sem,
    send_sem,
    recv_sem,
    rim_send_sem,
    rim_recv_sem,
    out_send_sem,
    out_recv_sem,
):
    me = lax.axis_index("freq")
    half = lax.axis_index("tm")
    last = GROUP - 1
    own_rows = own_tiles * 8
    window_rows = window * 8
    rim_rows = window_rows - own_rows
    is_last = me == last
    lane = lax.broadcasted_iota(jnp.int32, (TILES, LANES), 1)

    barrier = pltpu.get_barrier_semaphore()
    for mask in range(1, GROUP):
        pl.semaphore_signal(
            barrier, inc=1, device_id={"freq": butterfly_partner(me, mask)}, device_id_type=MESH
        )

    tables = [
        pltpu.make_async_copy(source, held, table_sem.at[index])
        for index, (source, held) in enumerate(
            ((bank_in, bank), (chan_shift_in, chan_shift), (sec_shift_in, sec_shift))
        )
    ]
    for table in tables:
        table.start()

    @pl.when(jnp.logical_and(is_last, half == 0))
    def _():
        for place in range(GROUP):
            pl.semaphore_signal(
                barrier, inc=1, device_id={"freq": place, "tm": 1}, device_id_type=MESH
            )

    def own_copy(rows):
        return pltpu.make_async_copy(
            samples_in.at[pl.ds(me * own_rows, rows), :],
            arrived.at[me, pl.ds(0, rows), :],
            local_sem,
        )

    def sent(target, rows):
        return pltpu.make_async_remote_copy(
            src_ref=samples_in.at[pl.ds(target * own_rows, rows), :],
            dst_ref=arrived.at[me, pl.ds(0, rows), :],
            send_sem=send_sem.at[target],
            recv_sem=recv_sem.at[me],
            device_id={"freq": target},
            device_id_type=MESH,
        )

    def awaited(source, rows):
        return pltpu.make_async_remote_copy(
            src_ref=samples_in.at[pl.ds(0, rows), :],
            dst_ref=arrived.at[source, pl.ds(0, rows), :],
            send_sem=send_sem.at[source],
            recv_sem=recv_sem.at[source],
            device_id={"freq": source},
            device_id_type=MESH,
        )

    def rim():
        return pltpu.make_async_remote_copy(
            src_ref=samples_in.at[pl.ds(0, rim_rows), :],
            dst_ref=arrived.at[me, pl.ds(own_rows, rim_rows), :],
            send_sem=rim_send_sem,
            recv_sem=rim_recv_sem.at[me],
            device_id={"freq": last, "tm": 0},
            device_id_type=MESH,
        )

    def rim_awaited(source):
        return pltpu.make_async_remote_copy(
            src_ref=samples_in.at[pl.ds(0, rim_rows), :],
            dst_ref=arrived.at[source, pl.ds(own_rows, rim_rows), :],
            send_sem=rim_send_sem,
            recv_sem=rim_recv_sem.at[source],
            device_id={"freq": last, "tm": 1},
            device_id_type=MESH,
        )

    @pl.when(is_last)
    def _():
        own_copy(own_rows).start()

    @pl.when(jnp.logical_not(is_last))
    def _():
        own_copy(window_rows).start()

    for source in range(GROUP):
        arrived[source, window_rows:, :] = jnp.zeros((TILES * 8 - window_rows, LANES), jnp.float32)

    @pl.when(jnp.logical_and(is_last, half == 1))
    def _():
        for source in range(GROUP):
            arrived[source, own_rows:window_rows, :] = jnp.zeros((rim_rows, LANES), jnp.float32)

    pl.semaphore_wait(barrier, GROUP - 1 + half)

    for mask in (6, 7, 4, 5, 2, 3, 1):
        target = butterfly_partner(me, mask)

        @pl.when(target == last)
        def _():
            sent(target, own_rows).start()

        @pl.when(target != last)
        def _():
            sent(target, window_rows).start()

    @pl.when(half == 1)
    def _():
        rim().start()

    for table in tables:
        table.wait()
    padded = jnp.concatenate([bank[...], jnp.zeros_like(bank[...])], axis=1)
    filters = padded.shape[0]
    for index in range(filters):
        spread = jnp.broadcast_to(padded[index : index + 1], (LANES, 2 * LANES))
        band = pltpu.roll(spread, 0, 1, stride=1, stride_axis=0)
        high, low = split(band)
        weights[pl.ds(index * LANES, LANES), :] = jnp.concatenate([high, high, low], axis=1)

    def take_source(source):
        for trial in range(2):
            rows = []
            for channel in range(8):
                raw = arrived[source, pl.ds(channel, TILES, stride=8), :]
                amount = chan_shift[trial, source * 8 + channel]
                rows.append(advanced(raw, next_sublane(raw), amount, lane))
            rows = butterflies(
                rows, lambda s, p: sec_shift[s, source * 16 + p * 2 + trial], lane
            )
            for position in range(8):
                start = pl.multiple_of((source * 16 + position * 2 + trial) * TILES, TILES)
                series[pl.ds(start, TILES), :] = rows[position]

    @pl.when(is_last)
    def _():
        own_copy(own_rows).wait()

    @pl.when(jnp.logical_not(is_last))
    def _():
        own_copy(window_rows).wait()

    for mask in (0, 1, 2, 3, 4, 5, 6, 7):
        source = butterfly_partner(me, mask)
        if mask:

            @pl.when(is_last)
            def _():
                awaited(source, own_rows).wait_recv()

            @pl.when(jnp.logical_not(is_last))
            def _():
                awaited(source, window_rows).wait_recv()

        @pl.when(jnp.logical_and(is_last, half == 0))
        def _():
            rim_awaited(source).wait_recv()

        take_source(source)

    @pl.loop(0, 16, unroll=4)
    def _(row):
        places = [pl.multiple_of((row + 16 * p) * TILES, TILES) for p in range(8)]
        rows = [series[pl.ds(place, TILES), :] for place in places]
        rows = butterflies(rows, lambda s, p: sec_shift[s + 3, row + 16 * p], lane)
        for place, values in zip(places, rows):
            series[pl.ds(place, TILES), :] = values

    tiles = [split(series[pl.ds(tile, LANES, stride=TILES), :]) for tile in range(own_tiles + 1)]
    inputs = jnp.concatenate(
        [
            jnp.concatenate(
                [tiles[tile + step][part] for part in (0, 1, 0) for step in range(2)], axis=1
            )
            for tile in range(own_tiles)
        ],
        axis=0,
    )
    filtered = lax.dot_general(
        weights[...], inputs, (((1,), (1,)), ((), ())), preferred_element_type=jnp.float32
    )
    sums = []
    for index in range(filters):
        part = filtered[index * LANES : (index + 1) * LANES]
        part = part * part
        total = part[:, :LANES]
        for tile in range(1, own_tiles):
            total = total + part[:, tile * LANES : (tile + 1) * LANES]
        sums.append(jnp.sum(total, axis=0, keepdims=True))
    energies[me] = jnp.concatenate(sums, axis=0)

    def energy_copy(target, place):
        return pltpu.make_async_remote_copy(
            src_ref=energies.at[me],
            dst_ref=energies.at[place],
            send_sem=out_send_sem.at[target],
            recv_sem=out_recv_sem.at[place],
            device_id={"freq": target},
            device_id_type=MESH,
        )

    for mask in (6, 7, 4, 5, 2, 3, 1):
        energy_copy(butterfly_partner(me, mask), me).start()
    for mask in (1, 2, 3, 4, 5, 6, 7):
        partner = butterfly_partner(me, mask)
        energy_copy(partner, partner).wait_recv()
    turn = ((GROUP - me) % GROUP) * 16
    per_block = GROUP // out.shape[1]
    for block in range(out.shape[1]):
        total = energies[block * per_block]
        for place in range(block * per_block + 1, (block + 1) * per_block):
            total = total + energies[place]
        total = pltpu.roll(total, turn, 1) * (1.0 / (BLOCK * GROUP * 8))
        for index in range(filters):
            out[index, block : block + 1, :] = total[index : index + 1, : out.shape[2]]

    for mask in range(1, GROUP):
        target = butterfly_partner(me, mask)

        @pl.when(target == last)
        def _():
            sent(target, own_rows).wait_send()

        @pl.when(target != last)
        def _():
            sent(target, window_rows).wait_send()

        energy_copy(target, me).wait_send()

    @pl.when(half == 1)
    def _():
        rim().wait_send()


def fused_body(intensity, channel_shift, section_shift, filter_bank):
    chan_dev, samples = intensity.shape
    tile_count = samples // LANES
    own_tiles = tile_count // GROUP
    reach = CHAN_MAX + SHIFT_UNIT * (2 ** section_shift.shape[0] - 1) + LANES
    window = own_tiles + -(-reach // LANES)
    filters = filter_bank.shape[0]
    blocks = samples // BLOCK
    by_tile = intensity.reshape(chan_dev, tile_count, LANES).transpose(1, 0, 2)
    by_tile = by_tile.reshape(tile_count * chan_dev, LANES)
    hbm = pl.BlockSpec(memory_space=pltpu.HBM)
    dma = pltpu.SemaphoreType.DMA
    maps = pl.pallas_call(
        functools.partial(kernel, own_tiles, window),
        out_shape=jax.ShapeDtypeStruct((filters, blocks, LANES // GROUP), jnp.float32),
        in_specs=[hbm] * 4,
        out_specs=pl.BlockSpec(memory_space=pltpu.VMEM),
        scratch_shapes=[
            pltpu.SMEM(channel_shift.shape[::-1], jnp.int32),
            pltpu.SMEM(section_shift.shape, jnp.int32),
            pltpu.VMEM(filter_bank.shape, jnp.float32),
            pltpu.VMEM((GROUP, TILES * chan_dev, LANES), jnp.float32),
            pltpu.VMEM((LANES * TILES, LANES), jnp.float32),
            pltpu.VMEM((filters * LANES, 6 * LANES), jnp.bfloat16),
            pltpu.VMEM((GROUP, filters, LANES), jnp.float32),
            dma((3,)),
            dma,
            dma((GROUP,)),
            dma((GROUP,)),
            dma,
            dma((GROUP,)),
            dma((GROUP,)),
            dma((GROUP,)),
        ],
        compiler_params=pltpu.CompilerParams(
            collective_id=0, has_side_effects=True, vmem_limit_bytes=60 * 2**20
        ),
    )(channel_shift.T, section_shift, filter_bank, by_tile)
    return maps.transpose(2, 0, 1)


def fits_fused(mesh, intensity, channel_shift, section_shift, filter_bank):
    groups, halves = mesh.shape["freq"], mesh.shape["tm"]
    samples = intensity.shape[1] // halves
    channels, trials_each = channel_shift.shape
    own = samples // groups
    reach = CHAN_MAX + SHIFT_UNIT * (2 ** section_shift.shape[0] - 1) + LANES
    return (
        groups == GROUP
        and halves == 2
        and channels == 8 * GROUP
        and trials_each == 2
        and filter_bank.shape == (8, LANES)
        and own % LANES == 0
        and BLOCK % own == 0
        and reach <= own
        and own + reach <= (TILES - 1) * LANES
    )


def solution(mesh):
    in_specs = (P(("beam", "freq"), "tm"), P(), P(), P())
    out_specs = P(("beam", "freq"), None, "tm")

    def whole(*arrays):
        chosen = fused_body if fits_fused(mesh, *arrays) else body
        return jax.shard_map(
            chosen, mesh=mesh, in_specs=in_specs, out_specs=out_specs, check_vma=False
        )(*arrays)

    return whole
```

```python
import functools

import jax
import jax.numpy as jnp
from jax import lax
from jax.experimental import pallas as pl
from jax.experimental.pallas import tpu as pltpu
from jax.sharding import PartitionSpec as P

SHIFT_UNIT = 3
CHAN_MAX = 15
BLOCK = 1024


def from_behind(block, axis, distance):
    devices = range(lax.axis_size(axis))
    route = [(i - distance, i) for i in devices if i - distance in devices]
    return lax.ppermute(block, axis, route)


def from_partner(array, axis, distance):
    return lax.ppermute(array, axis, [(i, i ^ 1 << distance) for i in range(lax.axis_size(axis))])


def shifted_rows(row_block, shifts, length):
    extra = row_block.shape[1] - length
    bit_count = max(extra, 0).bit_length()
    target = length + 2**bit_count - 1
    current = row_block
    if target > row_block.shape[1]:
        current = jnp.concatenate(
            [
                row_block,
                jnp.zeros((row_block.shape[0], target - row_block.shape[1]), row_block.dtype),
            ],
            axis=1,
        )
    for bit_index in range(bit_count - 1, -1, -1):
        step = 2**bit_index
        chosen = jnp.bitwise_and(jnp.right_shift(shifts, bit_index), 1)[:, None] == 1
        current = jnp.where(chosen, current[:, step:], current[:, : current.shape[1] - step])
    return current


def merge_bands(lower_band, upper_ext, shift_table, out_len):
    doubled_low = jnp.concatenate([lower_band, lower_band], axis=1)[:, :, :out_len]
    doubled_up = jnp.concatenate([upper_ext, upper_ext], axis=1)
    shifted = shifted_rows(
        doubled_up.reshape(-1, doubled_up.shape[2]), shift_table.reshape(-1), out_len
    )
    return doubled_low + shifted.reshape(doubled_low.shape)


def toeplitz_pair(filter_bank):
    tap_count = filter_bank.shape[1]
    lag_index = jnp.arange(tap_count)[:, None] - jnp.arange(tap_count)[None, :]
    toep_top = jnp.where(
        lag_index >= 0, jnp.take(filter_bank, jnp.clip(lag_index, 0, tap_count - 1), axis=1), 0.0
    )
    lag_later = lag_index + tap_count
    toep_low = jnp.where(
        lag_later < tap_count,
        jnp.take(filter_bank, jnp.clip(lag_later, 0, tap_count - 1), axis=1),
        0.0,
    )
    return (toep_top, toep_low)


def body(intensity, channel_shift, section_shift, filter_bank):
    chan_dev, samples = intensity.shape
    n_freq = lax.axis_size("freq")
    local_levels = chan_dev.bit_length() - 1
    freq_levels = n_freq.bit_length() - 1
    trials_each = channel_shift.shape[1]
    row_count = trials_each * chan_dev
    channels = chan_dev * n_freq
    freq_place = lax.axis_index("freq")
    own_section = lax.dynamic_slice_in_dim(section_shift, freq_place * row_count, row_count, 1)
    local_margin = SHIFT_UNIT * (2**local_levels - 1)
    margin = CHAN_MAX + local_margin
    rim_cols = from_behind(intensity[:, :margin], "tm", -1)
    extended = jnp.concatenate([intensity, rim_cols], axis=1)
    own_chan_shift = lax.dynamic_slice_in_dim(channel_shift, freq_place * chan_dev, chan_dev, 0)
    length = samples + margin - CHAN_MAX
    tree_rows = shifted_rows(
        jnp.repeat(extended, trials_each, axis=0), own_chan_shift.reshape(-1), length
    )
    tree_rows = tree_rows.reshape(chan_dev, trials_each, length)
    for section_index in range(local_levels):
        max_shift = SHIFT_UNIT * 2**section_index
        band_count, band_rows, span_len = tree_rows.shape
        lower_band = tree_rows[0::2]
        upper_band = tree_rows[1::2]
        out_len = span_len - max_shift
        upper_ext = upper_band
        shift_table = own_section[section_index].reshape(band_count // 2, 2 * band_rows)
        tree_rows = merge_bands(lower_band, upper_ext, shift_table, out_len)
    own_rows = tree_rows.reshape(row_count, samples)
    first_cross = 0
    for section_index in range(first_cross, freq_levels):
        max_shift = SHIFT_UNIT * 2 ** (local_levels + section_index)
        shift_table = own_section[local_levels + section_index]
        upper_bit = jnp.bitwise_and(jnp.right_shift(freq_place, section_index), 1)
        is_upper = upper_bit == 1
        sent_rows = own_rows
        partner_rows = from_partner(sent_rows, "freq", section_index)
        lower_band = jnp.where(is_upper, partner_rows, sent_rows)
        upper_band = jnp.where(is_upper, sent_rows, partner_rows)
        upper_rim = from_behind(upper_band[:, :max_shift], "tm", -1)
        upper_ext = jnp.concatenate([upper_band, upper_rim], axis=1)
        own_rows = lower_band + shifted_rows(upper_ext, shift_table, samples)
    tap_count = filter_bank.shape[1]
    filters = filter_bank.shape[0]
    tail_rows = from_behind(own_rows[:, : tap_count - 1], "tm", -1)
    padded = jnp.concatenate(
        [own_rows, tail_rows, jnp.zeros((row_count, 1), own_rows.dtype)], axis=1
    )
    first_half = padded[:, :samples].reshape(-1, tap_count)
    second_half = padded[:, tap_count:].reshape(-1, tap_count)
    toep_top, toep_low = toeplitz_pair(filter_bank)
    outputs = []
    for filter_index in range(filters):
        series = jnp.dot(
            first_half,
            toep_top[filter_index],
            precision=lax.Precision.HIGHEST,
            preferred_element_type=jnp.float32,
        )
        series = series + jnp.dot(
            second_half,
            toep_low[filter_index],
            precision=lax.Precision.HIGHEST,
            preferred_element_type=jnp.float32,
        )
        energy = jnp.sum((series * series).reshape(row_count, samples // BLOCK, BLOCK), axis=2)
        outputs.append(energy)
    return jnp.stack(outputs, axis=1) / (BLOCK * channels)


LANES = 128
GROUP = 8
TILES = 8
MESH = pl.DeviceIdType.MESH


def butterfly_partners(place):
    steps = []
    for bit in range(3):
        own = lax.rem(lax.div(place, 2**bit), 2)
        steps.append((1 - 2 * own) * 2**bit)
    partners = []
    for mask in range(GROUP):
        partner = place
        for bit in range(3):
            if mask >> bit & 1:
                partner = partner + steps[bit]
        partners.append(partner)
    return partners


def advanced(row, following, amount, lane):
    picked = jnp.where(lane < amount, following, row)
    return pltpu.roll(picked, jnp.bitwise_and(LANES - amount, LANES - 1), 1)


def next_sublane(row):
    return pltpu.roll(row, TILES - 1, 0)


def butterflies(rows, shift_of, lane):
    for section in range(3):
        gap = 2**section
        merged = list(rows)
        for low in range(8):
            if low & gap:
                continue
            up = rows[low + gap]
            following = next_sublane(up)
            merged[low] = rows[low] + advanced(up, following, shift_of(section, low), lane)
            merged[low + gap] = rows[low] + advanced(
                up, following, shift_of(section, low + gap), lane
            )
        rows = merged
    return rows


def split(values):
    high = values.astype(jnp.bfloat16)
    low = (values - high.astype(jnp.float32)).astype(jnp.bfloat16)
    return high, low


def kernel(
    own_tiles,
    window,
    chan_shift_in,
    sec_shift_in,
    bank_in,
    samples_in,
    out,
    chan_shift,
    sec_shift,
    bank,
    arrived,
    series,
    weights,
    energies,
    table_sem,
    local_sem,
    send_sem,
    recv_sem,
    rim_send_sem,
    rim_recv_sem,
    out_send_sem,
    out_recv_sem,
):
    me = lax.axis_index("freq")
    half = lax.axis_index("tm")
    last = GROUP - 1
    partners = butterfly_partners(me)
    own_rows = own_tiles * 8
    window_rows = window * 8
    rim_rows = window_rows - own_rows
    is_last = me == last
    lane = lax.broadcasted_iota(jnp.int32, (TILES, LANES), 1)

    barrier = pltpu.get_barrier_semaphore()
    for mask in range(1, GROUP):
        pl.semaphore_signal(
            barrier, inc=1, device_id={"freq": partners[mask]}, device_id_type=MESH
        )

    tables = [
        pltpu.make_async_copy(source, held, table_sem.at[index])
        for index, (source, held) in enumerate(
            ((bank_in, bank), (chan_shift_in, chan_shift), (sec_shift_in, sec_shift))
        )
    ]
    for table in tables:
        table.start()

    @pl.when(jnp.logical_and(is_last, half == 0))
    def _():
        for place in range(GROUP):
            pl.semaphore_signal(
                barrier, inc=1, device_id={"freq": place, "tm": 1}, device_id_type=MESH
            )

    def own_copy(rows):
        return pltpu.make_async_copy(
            samples_in.at[pl.ds(me * own_rows, rows), :],
            arrived.at[me, pl.ds(0, rows), :],
            local_sem,
        )

    def sent(target, rows):
        return pltpu.make_async_remote_copy(
            src_ref=samples_in.at[pl.ds(target * own_rows, rows), :],
            dst_ref=arrived.at[me, pl.ds(0, rows), :],
            send_sem=send_sem.at[target],
            recv_sem=recv_sem.at[me],
            device_id={"freq": target},
            device_id_type=MESH,
        )

    def awaited(source, rows):
        return pltpu.make_async_remote_copy(
            src_ref=samples_in.at[pl.ds(0, rows), :],
            dst_ref=arrived.at[source, pl.ds(0, rows), :],
            send_sem=send_sem.at[source],
            recv_sem=recv_sem.at[source],
            device_id={"freq": source},
            device_id_type=MESH,
        )

    def rim():
        return pltpu.make_async_remote_copy(
            src_ref=samples_in.at[pl.ds(0, rim_rows), :],
            dst_ref=arrived.at[me, pl.ds(own_rows, rim_rows), :],
            send_sem=rim_send_sem,
            recv_sem=rim_recv_sem.at[me],
            device_id={"freq": last, "tm": 0},
            device_id_type=MESH,
        )

    def rim_awaited(source):
        return pltpu.make_async_remote_copy(
            src_ref=samples_in.at[pl.ds(0, rim_rows), :],
            dst_ref=arrived.at[source, pl.ds(own_rows, rim_rows), :],
            send_sem=rim_send_sem,
            recv_sem=rim_recv_sem.at[source],
            device_id={"freq": last, "tm": 1},
            device_id_type=MESH,
        )

    @pl.when(is_last)
    def _():
        own_copy(own_rows).start()

    @pl.when(jnp.logical_not(is_last))
    def _():
        own_copy(window_rows).start()

    for source in range(GROUP):
        arrived[source, window_rows:, :] = jnp.zeros((TILES * 8 - window_rows, LANES), jnp.float32)

    @pl.when(jnp.logical_and(is_last, half == 1))
    def _():
        for source in range(GROUP):
            arrived[source, own_rows:window_rows, :] = jnp.zeros((rim_rows, LANES), jnp.float32)

    pl.semaphore_wait(barrier, GROUP - 1 + half)

    for mask in (6, 7, 4, 5, 2, 3, 1):
        target = partners[mask]

        @pl.when(target == last)
        def _():
            sent(target, own_rows).start()

        @pl.when(target != last)
        def _():
            sent(target, window_rows).start()

    @pl.when(half == 1)
    def _():
        rim().start()

    for table in tables:
        table.wait()
    padded = jnp.concatenate([bank[...], jnp.zeros_like(bank[...])], axis=1)
    filters = padded.shape[0]
    for index in range(filters):
        spread = jnp.broadcast_to(padded[index : index + 1], (LANES, 2 * LANES))
        band = pltpu.roll(spread, 0, 1, stride=1, stride_axis=0)
        high, low = split(band)
        weights[pl.ds(index * LANES, LANES), :] = jnp.concatenate([high, high, low], axis=1)

    def take_source(source):
        raws = [arrived[source, pl.ds(channel, TILES, stride=8), :] for channel in range(8)]
        nexts = [next_sublane(raw) for raw in raws]
        for trial in range(2):
            rows = []
            for channel in range(8):
                amount = chan_shift[trial, source * 8 + channel]
                rows.append(advanced(raws[channel], nexts[channel], amount, lane))
            rows = butterflies(
                rows, lambda s, p: sec_shift[s, source * 16 + p * 2 + trial], lane
            )
            for position in range(8):
                start = pl.multiple_of((source * 16 + position * 2 + trial) * TILES, TILES)
                series[pl.ds(start, TILES), :] = rows[position]

    @pl.when(is_last)
    def _():
        own_copy(own_rows).wait()

    @pl.when(jnp.logical_not(is_last))
    def _():
        own_copy(window_rows).wait()

    for mask in (0, 1, 2, 3, 4, 5, 6, 7):
        source = partners[mask]
        if mask:

            @pl.when(is_last)
            def _():
                awaited(source, own_rows).wait_recv()

            @pl.when(jnp.logical_not(is_last))
            def _():
                awaited(source, window_rows).wait_recv()

        @pl.when(jnp.logical_and(is_last, half == 0))
        def _():
            rim_awaited(source).wait_recv()

        take_source(source)

    @pl.loop(0, 16, unroll=4)
    def _(row):
        places = [pl.multiple_of((row + 16 * p) * TILES, TILES) for p in range(8)]
        rows = [series[pl.ds(place, TILES), :] for place in places]
        rows = butterflies(rows, lambda s, p: sec_shift[s + 3, row + 16 * p], lane)
        for place, values in zip(places, rows):
            series[pl.ds(place, TILES), :] = values

    tiles = [split(series[pl.ds(tile, LANES, stride=TILES), :]) for tile in range(own_tiles + 1)]
    inputs = jnp.concatenate(
        [
            jnp.concatenate(
                [tiles[tile + step][part] for part in (0, 1, 0) for step in range(2)], axis=1
            )
            for tile in range(own_tiles)
        ],
        axis=0,
    )
    filtered = lax.dot_general(
        weights[...], inputs, (((1,), (1,)), ((), ())), preferred_element_type=jnp.float32
    )
    sums = []
    for index in range(filters):
        part = filtered[index * LANES : (index + 1) * LANES]
        part = part * part
        total = part[:, :LANES]
        for tile in range(1, own_tiles):
            total = total + part[:, tile * LANES : (tile + 1) * LANES]
        sums.append(jnp.sum(total, axis=0, keepdims=True))
    energies[me] = jnp.concatenate(sums, axis=0)

    def energy_copy(target, place):
        return pltpu.make_async_remote_copy(
            src_ref=energies.at[me],
            dst_ref=energies.at[place],
            send_sem=out_send_sem.at[target],
            recv_sem=out_recv_sem.at[place],
            device_id={"freq": target},
            device_id_type=MESH,
        )

    for mask in (6, 7, 4, 5, 2, 3, 1):
        energy_copy(partners[mask], me).start()
    for mask in (1, 2, 3, 4, 5, 6, 7):
        partner = partners[mask]
        energy_copy(partner, partner).wait_recv()
    turn = lax.rem(GROUP - me, GROUP) * 16
    per_block = GROUP // out.shape[1]
    for block in range(out.shape[1]):
        total = energies[block * per_block]
        for place in range(block * per_block + 1, (block + 1) * per_block):
            total = total + energies[place]
        total = pltpu.roll(total, turn, 1) * (1.0 / (BLOCK * GROUP * 8))
        for index in range(filters):
            out[index, block : block + 1, :] = total[index : index + 1, : out.shape[2]]

    for mask in range(1, GROUP):
        target = partners[mask]

        @pl.when(target == last)
        def _():
            sent(target, own_rows).wait_send()

        @pl.when(target != last)
        def _():
            sent(target, window_rows).wait_send()

        energy_copy(target, me).wait_send()

    @pl.when(half == 1)
    def _():
        rim().wait_send()


def fused_body(intensity, channel_shift, section_shift, filter_bank):
    chan_dev, samples = intensity.shape
    tile_count = samples // LANES
    own_tiles = tile_count // GROUP
    reach = CHAN_MAX + SHIFT_UNIT * (2 ** section_shift.shape[0] - 1) + LANES
    window = own_tiles + -(-reach // LANES)
    filters = filter_bank.shape[0]
    blocks = samples // BLOCK
    by_tile = intensity.reshape(chan_dev, tile_count, LANES).transpose(1, 0, 2)
    by_tile = by_tile.reshape(tile_count * chan_dev, LANES)
    hbm = pl.BlockSpec(memory_space=pltpu.HBM)
    dma = pltpu.SemaphoreType.DMA
    maps = pl.pallas_call(
        functools.partial(kernel, own_tiles, window),
        out_shape=jax.ShapeDtypeStruct((filters, blocks, LANES // GROUP), jnp.float32),
        in_specs=[hbm] * 4,
        out_specs=pl.BlockSpec(memory_space=pltpu.VMEM),
        scratch_shapes=[
            pltpu.SMEM(channel_shift.shape[::-1], jnp.int32),
            pltpu.SMEM(section_shift.shape, jnp.int32),
            pltpu.VMEM(filter_bank.shape, jnp.float32),
            pltpu.VMEM((GROUP, TILES * chan_dev, LANES), jnp.float32),
            pltpu.VMEM((LANES * TILES, LANES), jnp.float32),
            pltpu.VMEM((filters * LANES, 6 * LANES), jnp.bfloat16),
            pltpu.VMEM((GROUP, filters, LANES), jnp.float32),
            dma((3,)),
            dma,
            dma((GROUP,)),
            dma((GROUP,)),
            dma,
            dma((GROUP,)),
            dma((GROUP,)),
            dma((GROUP,)),
        ],
        compiler_params=pltpu.CompilerParams(
            collective_id=0, has_side_effects=True, vmem_limit_bytes=60 * 2**20
        ),
    )(channel_shift.T, section_shift, filter_bank, by_tile)
    return maps.transpose(2, 0, 1)


def fits_fused(mesh, intensity, channel_shift, section_shift, filter_bank):
    groups, halves = mesh.shape["freq"], mesh.shape["tm"]
    samples = intensity.shape[1] // halves
    channels, trials_each = channel_shift.shape
    own = samples // groups
    reach = CHAN_MAX + SHIFT_UNIT * (2 ** section_shift.shape[0] - 1) + LANES
    return (
        groups == GROUP
        and halves == 2
        and channels == 8 * GROUP
        and trials_each == 2
        and filter_bank.shape == (8, LANES)
        and own % LANES == 0
        and BLOCK % own == 0
        and reach <= own
        and own + reach <= (TILES - 1) * LANES
    )


def solution(mesh):
    in_specs = (P(("beam", "freq"), "tm"), P(), P(), P())
    out_specs = P(("beam", "freq"), None, "tm")

    def whole(*arrays):
        chosen = fused_body if fits_fused(mesh, *arrays) else body
        return jax.shard_map(
            chosen, mesh=mesh, in_specs=in_specs, out_specs=out_specs, check_vma=False
        )(*arrays)

    return whole
```

```python
import functools

import jax
import jax.numpy as jnp
from jax import lax
from jax.experimental import pallas as pl
from jax.experimental.pallas import tpu as pltpu
from jax.sharding import PartitionSpec as P

SHIFT_UNIT = 3
CHAN_MAX = 15
BLOCK = 1024


def from_behind(block, axis, distance):
    devices = range(lax.axis_size(axis))
    route = [(i - distance, i) for i in devices if i - distance in devices]
    return lax.ppermute(block, axis, route)


def from_partner(array, axis, distance):
    return lax.ppermute(array, axis, [(i, i ^ 1 << distance) for i in range(lax.axis_size(axis))])


def shifted_rows(row_block, shifts, length):
    extra = row_block.shape[1] - length
    bit_count = max(extra, 0).bit_length()
    target = length + 2**bit_count - 1
    current = row_block
    if target > row_block.shape[1]:
        current = jnp.concatenate(
            [
                row_block,
                jnp.zeros((row_block.shape[0], target - row_block.shape[1]), row_block.dtype),
            ],
            axis=1,
        )
    for bit_index in range(bit_count - 1, -1, -1):
        step = 2**bit_index
        chosen = jnp.bitwise_and(jnp.right_shift(shifts, bit_index), 1)[:, None] == 1
        current = jnp.where(chosen, current[:, step:], current[:, : current.shape[1] - step])
    return current


def merge_bands(lower_band, upper_ext, shift_table, out_len):
    doubled_low = jnp.concatenate([lower_band, lower_band], axis=1)[:, :, :out_len]
    doubled_up = jnp.concatenate([upper_ext, upper_ext], axis=1)
    shifted = shifted_rows(
        doubled_up.reshape(-1, doubled_up.shape[2]), shift_table.reshape(-1), out_len
    )
    return doubled_low + shifted.reshape(doubled_low.shape)


def toeplitz_pair(filter_bank):
    tap_count = filter_bank.shape[1]
    lag_index = jnp.arange(tap_count)[:, None] - jnp.arange(tap_count)[None, :]
    toep_top = jnp.where(
        lag_index >= 0, jnp.take(filter_bank, jnp.clip(lag_index, 0, tap_count - 1), axis=1), 0.0
    )
    lag_later = lag_index + tap_count
    toep_low = jnp.where(
        lag_later < tap_count,
        jnp.take(filter_bank, jnp.clip(lag_later, 0, tap_count - 1), axis=1),
        0.0,
    )
    return (toep_top, toep_low)


def body(intensity, channel_shift, section_shift, filter_bank):
    chan_dev, samples = intensity.shape
    n_freq = lax.axis_size("freq")
    local_levels = chan_dev.bit_length() - 1
    freq_levels = n_freq.bit_length() - 1
    trials_each = channel_shift.shape[1]
    row_count = trials_each * chan_dev
    channels = chan_dev * n_freq
    freq_place = lax.axis_index("freq")
    own_section = lax.dynamic_slice_in_dim(section_shift, freq_place * row_count, row_count, 1)
    local_margin = SHIFT_UNIT * (2**local_levels - 1)
    margin = CHAN_MAX + local_margin
    rim_cols = from_behind(intensity[:, :margin], "tm", -1)
    extended = jnp.concatenate([intensity, rim_cols], axis=1)
    own_chan_shift = lax.dynamic_slice_in_dim(channel_shift, freq_place * chan_dev, chan_dev, 0)
    length = samples + margin - CHAN_MAX
    tree_rows = shifted_rows(
        jnp.repeat(extended, trials_each, axis=0), own_chan_shift.reshape(-1), length
    )
    tree_rows = tree_rows.reshape(chan_dev, trials_each, length)
    for section_index in range(local_levels):
        max_shift = SHIFT_UNIT * 2**section_index
        band_count, band_rows, span_len = tree_rows.shape
        lower_band = tree_rows[0::2]
        upper_band = tree_rows[1::2]
        out_len = span_len - max_shift
        upper_ext = upper_band
        shift_table = own_section[section_index].reshape(band_count // 2, 2 * band_rows)
        tree_rows = merge_bands(lower_band, upper_ext, shift_table, out_len)
    own_rows = tree_rows.reshape(row_count, samples)
    first_cross = 0
    for section_index in range(first_cross, freq_levels):
        max_shift = SHIFT_UNIT * 2 ** (local_levels + section_index)
        shift_table = own_section[local_levels + section_index]
        upper_bit = jnp.bitwise_and(jnp.right_shift(freq_place, section_index), 1)
        is_upper = upper_bit == 1
        sent_rows = own_rows
        partner_rows = from_partner(sent_rows, "freq", section_index)
        lower_band = jnp.where(is_upper, partner_rows, sent_rows)
        upper_band = jnp.where(is_upper, sent_rows, partner_rows)
        upper_rim = from_behind(upper_band[:, :max_shift], "tm", -1)
        upper_ext = jnp.concatenate([upper_band, upper_rim], axis=1)
        own_rows = lower_band + shifted_rows(upper_ext, shift_table, samples)
    tap_count = filter_bank.shape[1]
    filters = filter_bank.shape[0]
    tail_rows = from_behind(own_rows[:, : tap_count - 1], "tm", -1)
    padded = jnp.concatenate(
        [own_rows, tail_rows, jnp.zeros((row_count, 1), own_rows.dtype)], axis=1
    )
    first_half = padded[:, :samples].reshape(-1, tap_count)
    second_half = padded[:, tap_count:].reshape(-1, tap_count)
    toep_top, toep_low = toeplitz_pair(filter_bank)
    outputs = []
    for filter_index in range(filters):
        series = jnp.dot(
            first_half,
            toep_top[filter_index],
            precision=lax.Precision.HIGHEST,
            preferred_element_type=jnp.float32,
        )
        series = series + jnp.dot(
            second_half,
            toep_low[filter_index],
            precision=lax.Precision.HIGHEST,
            preferred_element_type=jnp.float32,
        )
        energy = jnp.sum((series * series).reshape(row_count, samples // BLOCK, BLOCK), axis=2)
        outputs.append(energy)
    return jnp.stack(outputs, axis=1) / (BLOCK * channels)


LANES = 128
GROUP = 8
TILES = 8
MESH = pl.DeviceIdType.MESH


def butterfly_partners(place):
    steps = []
    for bit in range(3):
        own = lax.rem(lax.div(place, 2**bit), 2)
        steps.append((1 - 2 * own) * 2**bit)
    partners = []
    for mask in range(GROUP):
        partner = place
        for bit in range(3):
            if mask >> bit & 1:
                partner = partner + steps[bit]
        partners.append(partner)
    return partners


def advanced(row, following, amount, lane):
    picked = jnp.where(lane < amount, following, row)
    return pltpu.roll(picked, jnp.bitwise_and(LANES - amount, LANES - 1), 1)


def next_sublane(row):
    return pltpu.roll(row, TILES - 1, 0)


def butterflies(rows, shift_of, lane):
    for section in range(3):
        gap = 2**section
        merged = list(rows)
        for low in range(8):
            if low & gap:
                continue
            up = rows[low + gap]
            following = next_sublane(up)
            merged[low] = rows[low] + advanced(up, following, shift_of(section, low), lane)
            merged[low + gap] = rows[low] + advanced(
                up, following, shift_of(section, low + gap), lane
            )
        rows = merged
    return rows


def split(values):
    high = values.astype(jnp.bfloat16)
    low = (values - high.astype(jnp.float32)).astype(jnp.bfloat16)
    return high, low


def kernel(
    own_tiles,
    window,
    chan_shift_in,
    sec_shift_in,
    bank_in,
    samples_in,
    out,
    chan_shift,
    sec_shift,
    bank,
    arrived,
    series,
    weights,
    energies,
    table_sem,
    local_sem,
    send_sem,
    recv_sem,
    rim_send_sem,
    rim_recv_sem,
    out_send_sem,
    out_recv_sem,
):
    me = lax.axis_index("freq")
    half = lax.axis_index("tm")
    last = GROUP - 1
    partners = butterfly_partners(me)
    own_rows = own_tiles * 8
    window_rows = window * 8
    rim_rows = window_rows - own_rows
    is_last = me == last
    lane = lax.broadcasted_iota(jnp.int32, (TILES, LANES), 1)

    barrier = pltpu.get_barrier_semaphore()
    for mask in range(1, GROUP):
        pl.semaphore_signal(
            barrier, inc=1, device_id={"freq": partners[mask]}, device_id_type=MESH
        )

    tables = [
        pltpu.make_async_copy(source, held, table_sem.at[index])
        for index, (source, held) in enumerate(
            ((bank_in, bank), (chan_shift_in, chan_shift), (sec_shift_in, sec_shift))
        )
    ]
    for table in tables:
        table.start()

    @pl.when(jnp.logical_and(is_last, half == 0))
    def _():
        for place in range(GROUP):
            pl.semaphore_signal(
                barrier, inc=1, device_id={"freq": place, "tm": 1}, device_id_type=MESH
            )

    def own_copy(rows):
        return pltpu.make_async_copy(
            samples_in.at[pl.ds(me * own_rows, rows), :],
            arrived.at[me, pl.ds(0, rows), :],
            local_sem,
        )

    def sent(target, rows):
        return pltpu.make_async_remote_copy(
            src_ref=samples_in.at[pl.ds(target * own_rows, rows), :],
            dst_ref=arrived.at[me, pl.ds(0, rows), :],
            send_sem=send_sem.at[target],
            recv_sem=recv_sem.at[me],
            device_id={"freq": target},
            device_id_type=MESH,
        )

    def awaited(source, rows):
        return pltpu.make_async_remote_copy(
            src_ref=samples_in.at[pl.ds(0, rows), :],
            dst_ref=arrived.at[source, pl.ds(0, rows), :],
            send_sem=send_sem.at[source],
            recv_sem=recv_sem.at[source],
            device_id={"freq": source},
            device_id_type=MESH,
        )

    def rim():
        return pltpu.make_async_remote_copy(
            src_ref=samples_in.at[pl.ds(0, rim_rows), :],
            dst_ref=arrived.at[me, pl.ds(own_rows, rim_rows), :],
            send_sem=rim_send_sem,
            recv_sem=rim_recv_sem.at[me],
            device_id={"freq": last, "tm": 0},
            device_id_type=MESH,
        )

    def rim_awaited(source):
        return pltpu.make_async_remote_copy(
            src_ref=samples_in.at[pl.ds(0, rim_rows), :],
            dst_ref=arrived.at[source, pl.ds(own_rows, rim_rows), :],
            send_sem=rim_send_sem,
            recv_sem=rim_recv_sem.at[source],
            device_id={"freq": last, "tm": 1},
            device_id_type=MESH,
        )

    @pl.when(is_last)
    def _():
        own_copy(own_rows).start()

    @pl.when(jnp.logical_not(is_last))
    def _():
        own_copy(window_rows).start()

    for source in range(GROUP):
        arrived[source, window_rows:, :] = jnp.zeros((TILES * 8 - window_rows, LANES), jnp.float32)

    @pl.when(jnp.logical_and(is_last, half == 1))
    def _():
        for source in range(GROUP):
            arrived[source, own_rows:window_rows, :] = jnp.zeros((rim_rows, LANES), jnp.float32)

    pl.semaphore_wait(barrier, GROUP - 1 + half)

    for mask in (6, 7, 4, 5, 2, 3, 1):
        target = partners[mask]

        @pl.when(target == last)
        def _():
            sent(target, own_rows).start()

        @pl.when(target != last)
        def _():
            sent(target, window_rows).start()

    @pl.when(half == 1)
    def _():
        rim().start()

    for table in tables:
        table.wait()
    padded = jnp.concatenate([bank[...], jnp.zeros_like(bank[...])], axis=1)
    filters = padded.shape[0]
    for index in range(filters):
        spread = jnp.broadcast_to(padded[index : index + 1], (LANES, 2 * LANES))
        band = pltpu.roll(spread, 0, 1, stride=1, stride_axis=0)
        high, low = split(band)
        weights[pl.ds(index * LANES, LANES), :] = jnp.concatenate([high, high, low], axis=1)

    def take_source(source):
        raws = [arrived[source, pl.ds(channel, TILES, stride=8), :] for channel in range(8)]
        nexts = [next_sublane(raw) for raw in raws]
        for trial in range(2):
            rows = []
            for channel in range(8):
                amount = chan_shift[trial, source * 8 + channel]
                rows.append(advanced(raws[channel], nexts[channel], amount, lane))
            rows = butterflies(
                rows, lambda s, p: sec_shift[s, source * 16 + p * 2 + trial], lane
            )
            for position in range(8):
                start = pl.multiple_of((source * 16 + position * 2 + trial) * TILES, TILES)
                series[pl.ds(start, TILES), :] = rows[position]

    @pl.when(is_last)
    def _():
        own_copy(own_rows).wait()

    @pl.when(jnp.logical_not(is_last))
    def _():
        own_copy(window_rows).wait()

    for mask in (0, 1, 2, 3, 4, 5, 6, 7):
        source = partners[mask]
        if mask:

            @pl.when(is_last)
            def _():
                awaited(source, own_rows).wait_recv()

            @pl.when(jnp.logical_not(is_last))
            def _():
                awaited(source, window_rows).wait_recv()

        @pl.when(jnp.logical_and(is_last, half == 0))
        def _():
            rim_awaited(source).wait_recv()

        take_source(source)

    @pl.loop(0, 16, unroll=8)
    def _(row):
        places = [pl.multiple_of((row + 16 * p) * TILES, TILES) for p in range(8)]
        rows = [series[pl.ds(place, TILES), :] for place in places]
        rows = butterflies(rows, lambda s, p: sec_shift[s + 3, row + 16 * p], lane)
        for place, values in zip(places, rows):
            series[pl.ds(place, TILES), :] = values

    tiles = [split(series[pl.ds(tile, LANES, stride=TILES), :]) for tile in range(own_tiles + 1)]
    sums = [None] * filters
    for first in range(0, own_tiles, 2):
        inputs = jnp.concatenate(
            [
                jnp.concatenate(
                    [tiles[tile + step][part] for part in (0, 1, 0) for step in range(2)], axis=1
                )
                for tile in range(first, first + 2)
            ],
            axis=0,
        )
        filtered = lax.dot_general(
            weights[...], inputs, (((1,), (1,)), ((), ())), preferred_element_type=jnp.float32
        )
        for index in range(filters):
            part = filtered[index * LANES : (index + 1) * LANES]
            part = part * part
            total = jnp.sum(part[:, :LANES] + part[:, LANES:], axis=0, keepdims=True)
            sums[index] = total if first == 0 else sums[index] + total
    energies[me] = jnp.concatenate(sums, axis=0)

    def energy_copy(target, place):
        return pltpu.make_async_remote_copy(
            src_ref=energies.at[me],
            dst_ref=energies.at[place],
            send_sem=out_send_sem.at[target],
            recv_sem=out_recv_sem.at[place],
            device_id={"freq": target},
            device_id_type=MESH,
        )

    for mask in (6, 7, 4, 5, 2, 3, 1):
        energy_copy(partners[mask], me).start()
    for mask in (1, 2, 3, 4, 5, 6, 7):
        partner = partners[mask]
        energy_copy(partner, partner).wait_recv()
    turn = lax.rem(GROUP - me, GROUP) * 16
    per_block = GROUP // out.shape[1]
    for block in range(out.shape[1]):
        total = energies[block * per_block]
        for place in range(block * per_block + 1, (block + 1) * per_block):
            total = total + energies[place]
        total = pltpu.roll(total, turn, 1) * (1.0 / (BLOCK * GROUP * 8))
        for index in range(filters):
            out[index, block : block + 1, :] = total[index : index + 1, : out.shape[2]]

    for mask in range(1, GROUP):
        target = partners[mask]

        @pl.when(target == last)
        def _():
            sent(target, own_rows).wait_send()

        @pl.when(target != last)
        def _():
            sent(target, window_rows).wait_send()

        energy_copy(target, me).wait_send()

    @pl.when(half == 1)
    def _():
        rim().wait_send()


def fused_body(intensity, channel_shift, section_shift, filter_bank):
    chan_dev, samples = intensity.shape
    tile_count = samples // LANES
    own_tiles = tile_count // GROUP
    reach = CHAN_MAX + SHIFT_UNIT * (2 ** section_shift.shape[0] - 1) + LANES
    window = own_tiles + -(-reach // LANES)
    filters = filter_bank.shape[0]
    blocks = samples // BLOCK
    by_tile = intensity.reshape(chan_dev, tile_count, LANES).transpose(1, 0, 2)
    by_tile = by_tile.reshape(tile_count * chan_dev, LANES)
    hbm = pl.BlockSpec(memory_space=pltpu.HBM)
    dma = pltpu.SemaphoreType.DMA
    maps = pl.pallas_call(
        functools.partial(kernel, own_tiles, window),
        out_shape=jax.ShapeDtypeStruct((filters, blocks, LANES // GROUP), jnp.float32),
        in_specs=[hbm] * 4,
        out_specs=pl.BlockSpec(memory_space=pltpu.VMEM),
        scratch_shapes=[
            pltpu.SMEM(channel_shift.shape[::-1], jnp.int32),
            pltpu.SMEM(section_shift.shape, jnp.int32),
            pltpu.VMEM(filter_bank.shape, jnp.float32),
            pltpu.VMEM((GROUP, TILES * chan_dev, LANES), jnp.float32),
            pltpu.VMEM((LANES * TILES, LANES), jnp.float32),
            pltpu.VMEM((filters * LANES, 6 * LANES), jnp.bfloat16),
            pltpu.VMEM((GROUP, filters, LANES), jnp.float32),
            dma((3,)),
            dma,
            dma((GROUP,)),
            dma((GROUP,)),
            dma,
            dma((GROUP,)),
            dma((GROUP,)),
            dma((GROUP,)),
        ],
        compiler_params=pltpu.CompilerParams(
            collective_id=0, has_side_effects=True, vmem_limit_bytes=60 * 2**20
        ),
    )(channel_shift.T, section_shift, filter_bank, by_tile)
    return maps.transpose(2, 0, 1)


def fits_fused(mesh, intensity, channel_shift, section_shift, filter_bank):
    groups, halves = mesh.shape["freq"], mesh.shape["tm"]
    samples = intensity.shape[1] // halves
    channels, trials_each = channel_shift.shape
    own = samples // groups
    reach = CHAN_MAX + SHIFT_UNIT * (2 ** section_shift.shape[0] - 1) + LANES
    return (
        groups == GROUP
        and halves == 2
        and channels == 8 * GROUP
        and trials_each == 2
        and filter_bank.shape == (8, LANES)
        and own % (2 * LANES) == 0
        and BLOCK % own == 0
        and reach <= own
        and own + reach <= (TILES - 1) * LANES
    )


def solution(mesh):
    in_specs = (P(("beam", "freq"), "tm"), P(), P(), P())
    out_specs = P(("beam", "freq"), None, "tm")

    def whole(*arrays):
        chosen = fused_body if fits_fused(mesh, *arrays) else body
        return jax.shard_map(
            chosen, mesh=mesh, in_specs=in_specs, out_specs=out_specs, check_vma=False
        )(*arrays)

    return whole
```

```python
import functools

import jax
import jax.numpy as jnp
from jax import lax
from jax.experimental import pallas as pl
from jax.experimental.pallas import tpu as pltpu
from jax.sharding import PartitionSpec as P

SHIFT_UNIT = 3
CHAN_MAX = 15
BLOCK = 1024


def from_behind(block, axis, distance):
    devices = range(lax.axis_size(axis))
    route = [(i - distance, i) for i in devices if i - distance in devices]
    return lax.ppermute(block, axis, route)


def from_partner(array, axis, distance):
    return lax.ppermute(array, axis, [(i, i ^ 1 << distance) for i in range(lax.axis_size(axis))])


def shifted_rows(row_block, shifts, length):
    extra = row_block.shape[1] - length
    bit_count = max(extra, 0).bit_length()
    target = length + 2**bit_count - 1
    current = row_block
    if target > row_block.shape[1]:
        current = jnp.concatenate(
            [
                row_block,
                jnp.zeros((row_block.shape[0], target - row_block.shape[1]), row_block.dtype),
            ],
            axis=1,
        )
    for bit_index in range(bit_count - 1, -1, -1):
        step = 2**bit_index
        chosen = jnp.bitwise_and(jnp.right_shift(shifts, bit_index), 1)[:, None] == 1
        current = jnp.where(chosen, current[:, step:], current[:, : current.shape[1] - step])
    return current


def merge_bands(lower_band, upper_ext, shift_table, out_len):
    doubled_low = jnp.concatenate([lower_band, lower_band], axis=1)[:, :, :out_len]
    doubled_up = jnp.concatenate([upper_ext, upper_ext], axis=1)
    shifted = shifted_rows(
        doubled_up.reshape(-1, doubled_up.shape[2]), shift_table.reshape(-1), out_len
    )
    return doubled_low + shifted.reshape(doubled_low.shape)


def toeplitz_pair(filter_bank):
    tap_count = filter_bank.shape[1]
    lag_index = jnp.arange(tap_count)[:, None] - jnp.arange(tap_count)[None, :]
    toep_top = jnp.where(
        lag_index >= 0, jnp.take(filter_bank, jnp.clip(lag_index, 0, tap_count - 1), axis=1), 0.0
    )
    lag_later = lag_index + tap_count
    toep_low = jnp.where(
        lag_later < tap_count,
        jnp.take(filter_bank, jnp.clip(lag_later, 0, tap_count - 1), axis=1),
        0.0,
    )
    return (toep_top, toep_low)


def body(intensity, channel_shift, section_shift, filter_bank):
    chan_dev, samples = intensity.shape
    n_freq = lax.axis_size("freq")
    local_levels = chan_dev.bit_length() - 1
    freq_levels = n_freq.bit_length() - 1
    trials_each = channel_shift.shape[1]
    row_count = trials_each * chan_dev
    channels = chan_dev * n_freq
    freq_place = lax.axis_index("freq")
    own_section = lax.dynamic_slice_in_dim(section_shift, freq_place * row_count, row_count, 1)
    local_margin = SHIFT_UNIT * (2**local_levels - 1)
    margin = CHAN_MAX + local_margin
    rim_cols = from_behind(intensity[:, :margin], "tm", -1)
    extended = jnp.concatenate([intensity, rim_cols], axis=1)
    own_chan_shift = lax.dynamic_slice_in_dim(channel_shift, freq_place * chan_dev, chan_dev, 0)
    length = samples + margin - CHAN_MAX
    tree_rows = shifted_rows(
        jnp.repeat(extended, trials_each, axis=0), own_chan_shift.reshape(-1), length
    )
    tree_rows = tree_rows.reshape(chan_dev, trials_each, length)
    for section_index in range(local_levels):
        max_shift = SHIFT_UNIT * 2**section_index
        band_count, band_rows, span_len = tree_rows.shape
        lower_band = tree_rows[0::2]
        upper_band = tree_rows[1::2]
        out_len = span_len - max_shift
        upper_ext = upper_band
        shift_table = own_section[section_index].reshape(band_count // 2, 2 * band_rows)
        tree_rows = merge_bands(lower_band, upper_ext, shift_table, out_len)
    own_rows = tree_rows.reshape(row_count, samples)
    first_cross = 0
    for section_index in range(first_cross, freq_levels):
        max_shift = SHIFT_UNIT * 2 ** (local_levels + section_index)
        shift_table = own_section[local_levels + section_index]
        upper_bit = jnp.bitwise_and(jnp.right_shift(freq_place, section_index), 1)
        is_upper = upper_bit == 1
        sent_rows = own_rows
        partner_rows = from_partner(sent_rows, "freq", section_index)
        lower_band = jnp.where(is_upper, partner_rows, sent_rows)
        upper_band = jnp.where(is_upper, sent_rows, partner_rows)
        upper_rim = from_behind(upper_band[:, :max_shift], "tm", -1)
        upper_ext = jnp.concatenate([upper_band, upper_rim], axis=1)
        own_rows = lower_band + shifted_rows(upper_ext, shift_table, samples)
    tap_count = filter_bank.shape[1]
    filters = filter_bank.shape[0]
    tail_rows = from_behind(own_rows[:, : tap_count - 1], "tm", -1)
    padded = jnp.concatenate(
        [own_rows, tail_rows, jnp.zeros((row_count, 1), own_rows.dtype)], axis=1
    )
    first_half = padded[:, :samples].reshape(-1, tap_count)
    second_half = padded[:, tap_count:].reshape(-1, tap_count)
    toep_top, toep_low = toeplitz_pair(filter_bank)
    outputs = []
    for filter_index in range(filters):
        series = jnp.dot(
            first_half,
            toep_top[filter_index],
            precision=lax.Precision.HIGHEST,
            preferred_element_type=jnp.float32,
        )
        series = series + jnp.dot(
            second_half,
            toep_low[filter_index],
            precision=lax.Precision.HIGHEST,
            preferred_element_type=jnp.float32,
        )
        energy = jnp.sum((series * series).reshape(row_count, samples // BLOCK, BLOCK), axis=2)
        outputs.append(energy)
    return jnp.stack(outputs, axis=1) / (BLOCK * channels)


LANES = 128
GROUP = 8
TILES = 8
MESH = pl.DeviceIdType.MESH


def butterfly_partners(place):
    steps = []
    for bit in range(3):
        own = lax.rem(lax.div(place, 2**bit), 2)
        steps.append((1 - 2 * own) * 2**bit)
    partners = []
    for mask in range(GROUP):
        partner = place
        for bit in range(3):
            if mask >> bit & 1:
                partner = partner + steps[bit]
        partners.append(partner)
    return partners


def advanced(row, following, amount, lane):
    picked = jnp.where(lane < amount, following, row)
    return pltpu.roll(picked, jnp.bitwise_and(LANES - amount, LANES - 1), 1)


def next_sublane(row):
    return pltpu.roll(row, TILES - 1, 0)


def butterflies(rows, shift_of, lane):
    for section in range(3):
        gap = 2**section
        merged = list(rows)
        for low in range(8):
            if low & gap:
                continue
            up = rows[low + gap]
            following = next_sublane(up)
            merged[low] = rows[low] + advanced(up, following, shift_of(section, low), lane)
            merged[low + gap] = rows[low] + advanced(
                up, following, shift_of(section, low + gap), lane
            )
        rows = merged
    return rows


def split(values):
    high = values.astype(jnp.bfloat16)
    low = (values - high.astype(jnp.float32)).astype(jnp.bfloat16)
    return high, low


def kernel(
    own_tiles,
    window,
    chan_shift_in,
    sec_shift_in,
    bank_in,
    samples_in,
    out,
    chan_shift,
    sec_shift,
    bank,
    arrived,
    series,
    weights,
    energies,
    table_sem,
    local_sem,
    send_sem,
    recv_sem,
    rim_send_sem,
    rim_recv_sem,
    out_send_sem,
    out_recv_sem,
):
    me = lax.axis_index("freq")
    half = lax.axis_index("tm")
    last = GROUP - 1
    partners = butterfly_partners(me)
    own_rows = own_tiles * 8
    window_rows = window * 8
    rim_rows = window_rows - own_rows
    is_last = me == last
    lane = lax.broadcasted_iota(jnp.int32, (TILES, LANES), 1)

    barrier = pltpu.get_barrier_semaphore()
    for mask in range(1, GROUP):
        pl.semaphore_signal(
            barrier, inc=1, device_id={"freq": partners[mask]}, device_id_type=MESH
        )

    tables = [
        pltpu.make_async_copy(source, held, table_sem.at[index])
        for index, (source, held) in enumerate(
            ((bank_in, bank), (chan_shift_in, chan_shift), (sec_shift_in, sec_shift))
        )
    ]
    for table in tables:
        table.start()

    @pl.when(jnp.logical_and(is_last, half == 0))
    def _():
        for place in range(GROUP):
            pl.semaphore_signal(
                barrier, inc=1, device_id={"freq": place, "tm": 1}, device_id_type=MESH
            )

    def own_copy(rows):
        return pltpu.make_async_copy(
            samples_in.at[pl.ds(me * own_rows, rows), :],
            arrived.at[me, pl.ds(0, rows), :],
            local_sem,
        )

    def sent(target, rows):
        return pltpu.make_async_remote_copy(
            src_ref=samples_in.at[pl.ds(target * own_rows, rows), :],
            dst_ref=arrived.at[me, pl.ds(0, rows), :],
            send_sem=send_sem.at[target],
            recv_sem=recv_sem.at[me],
            device_id={"freq": target},
            device_id_type=MESH,
        )

    def awaited(source, rows):
        return pltpu.make_async_remote_copy(
            src_ref=samples_in.at[pl.ds(0, rows), :],
            dst_ref=arrived.at[source, pl.ds(0, rows), :],
            send_sem=send_sem.at[source],
            recv_sem=recv_sem.at[source],
            device_id={"freq": source},
            device_id_type=MESH,
        )

    def rim():
        return pltpu.make_async_remote_copy(
            src_ref=samples_in.at[pl.ds(0, rim_rows), :],
            dst_ref=arrived.at[me, pl.ds(own_rows, rim_rows), :],
            send_sem=rim_send_sem,
            recv_sem=rim_recv_sem.at[me],
            device_id={"freq": last, "tm": 0},
            device_id_type=MESH,
        )

    def rim_awaited(source):
        return pltpu.make_async_remote_copy(
            src_ref=samples_in.at[pl.ds(0, rim_rows), :],
            dst_ref=arrived.at[source, pl.ds(own_rows, rim_rows), :],
            send_sem=rim_send_sem,
            recv_sem=rim_recv_sem.at[source],
            device_id={"freq": last, "tm": 1},
            device_id_type=MESH,
        )

    @pl.when(is_last)
    def _():
        own_copy(own_rows).start()

    @pl.when(jnp.logical_not(is_last))
    def _():
        own_copy(window_rows).start()

    for source in range(GROUP):
        arrived[source, window_rows:, :] = jnp.zeros(
            (TILES * 8 + 8 - window_rows, LANES), jnp.float32
        )

    @pl.when(jnp.logical_and(is_last, half == 1))
    def _():
        for source in range(GROUP):
            arrived[source, own_rows:window_rows, :] = jnp.zeros((rim_rows, LANES), jnp.float32)

    pl.semaphore_wait(barrier, GROUP - 1 + half)

    for mask in (6, 7, 4, 5, 2, 3, 1):
        target = partners[mask]

        @pl.when(target == last)
        def _():
            sent(target, own_rows).start()

        @pl.when(target != last)
        def _():
            sent(target, window_rows).start()

    @pl.when(half == 1)
    def _():
        rim().start()

    for table in tables:
        table.wait()
    padded = jnp.concatenate([bank[...], jnp.zeros_like(bank[...])], axis=1)
    filters = padded.shape[0]
    for index in range(filters):
        spread = jnp.broadcast_to(padded[index : index + 1], (LANES, 2 * LANES))
        band = pltpu.roll(spread, 0, 1, stride=1, stride_axis=0)
        high, low = split(band)
        weights[pl.ds(index * LANES, LANES), :] = jnp.concatenate([high, high, low], axis=1)

    def take_source(source):
        raws = [arrived[source, pl.ds(channel, TILES, stride=8), :] for channel in range(8)]
        nexts = [arrived[source, pl.ds(channel + 8, TILES, stride=8), :] for channel in range(8)]
        for trial in range(2):
            rows = []
            for channel in range(8):
                amount = chan_shift[trial, source * 8 + channel]
                rows.append(advanced(raws[channel], nexts[channel], amount, lane))
            rows = butterflies(
                rows, lambda s, p: sec_shift[s, source * 16 + p * 2 + trial], lane
            )
            for position in range(8):
                start = pl.multiple_of((source * 16 + position * 2 + trial) * TILES, TILES)
                series[pl.ds(start, TILES), :] = rows[position]

    @pl.when(is_last)
    def _():
        own_copy(own_rows).wait()

    @pl.when(jnp.logical_not(is_last))
    def _():
        own_copy(window_rows).wait()

    for mask in (0, 1, 2, 3, 4, 5, 6, 7):
        source = partners[mask]
        if mask:

            @pl.when(is_last)
            def _():
                awaited(source, own_rows).wait_recv()

            @pl.when(jnp.logical_not(is_last))
            def _():
                awaited(source, window_rows).wait_recv()

        @pl.when(jnp.logical_and(is_last, half == 0))
        def _():
            rim_awaited(source).wait_recv()

        take_source(source)

    @pl.loop(0, 16, unroll=8)
    def _(row):
        places = [pl.multiple_of((row + 16 * p) * TILES, TILES) for p in range(8)]
        rows = [series[pl.ds(place, TILES), :] for place in places]
        rows = butterflies(rows, lambda s, p: sec_shift[s + 3, row + 16 * p], lane)
        for place, values in zip(places, rows):
            series[pl.ds(place, TILES), :] = values

    tiles = [split(series[pl.ds(tile, LANES, stride=TILES), :]) for tile in range(own_tiles + 1)]
    sums = [None] * filters
    for first in range(0, own_tiles, 2):
        inputs = jnp.concatenate(
            [
                jnp.concatenate(
                    [tiles[tile + step][part] for part in (0, 1, 0) for step in range(2)], axis=1
                )
                for tile in range(first, first + 2)
            ],
            axis=0,
        )
        filtered = lax.dot_general(
            weights[...], inputs, (((1,), (1,)), ((), ())), preferred_element_type=jnp.float32
        )
        for index in range(filters):
            part = filtered[index * LANES : (index + 1) * LANES]
            part = part * part
            total = jnp.sum(part[:, :LANES] + part[:, LANES:], axis=0, keepdims=True)
            sums[index] = total if first == 0 else sums[index] + total
    energies[me] = jnp.concatenate(sums, axis=0)

    def energy_copy(target, place):
        return pltpu.make_async_remote_copy(
            src_ref=energies.at[me],
            dst_ref=energies.at[place],
            send_sem=out_send_sem.at[target],
            recv_sem=out_recv_sem.at[place],
            device_id={"freq": target},
            device_id_type=MESH,
        )

    for mask in (6, 7, 4, 5, 2, 3, 1):
        energy_copy(partners[mask], me).start()
    for mask in (1, 2, 3, 4, 5, 6, 7):
        partner = partners[mask]
        energy_copy(partner, partner).wait_recv()
    turn = lax.rem(GROUP - me, GROUP) * 16
    per_block = GROUP // out.shape[1]
    for block in range(out.shape[1]):
        total = energies[block * per_block]
        for place in range(block * per_block + 1, (block + 1) * per_block):
            total = total + energies[place]
        total = pltpu.roll(total, turn, 1) * (1.0 / (BLOCK * GROUP * 8))
        for index in range(filters):
            out[index, block : block + 1, :] = total[index : index + 1, : out.shape[2]]

    for mask in range(1, GROUP):
        target = partners[mask]

        @pl.when(target == last)
        def _():
            sent(target, own_rows).wait_send()

        @pl.when(target != last)
        def _():
            sent(target, window_rows).wait_send()

        energy_copy(target, me).wait_send()

    @pl.when(half == 1)
    def _():
        rim().wait_send()


def fused_body(intensity, channel_shift, section_shift, filter_bank):
    chan_dev, samples = intensity.shape
    tile_count = samples // LANES
    own_tiles = tile_count // GROUP
    reach = CHAN_MAX + SHIFT_UNIT * (2 ** section_shift.shape[0] - 1) + LANES
    window = own_tiles + -(-reach // LANES)
    filters = filter_bank.shape[0]
    blocks = samples // BLOCK
    by_tile = intensity.reshape(chan_dev, tile_count, LANES).transpose(1, 0, 2)
    by_tile = by_tile.reshape(tile_count * chan_dev, LANES)
    hbm = pl.BlockSpec(memory_space=pltpu.HBM)
    dma = pltpu.SemaphoreType.DMA
    maps = pl.pallas_call(
        functools.partial(kernel, own_tiles, window),
        out_shape=jax.ShapeDtypeStruct((filters, blocks, LANES // GROUP), jnp.float32),
        in_specs=[hbm] * 4,
        out_specs=pl.BlockSpec(memory_space=pltpu.VMEM),
        scratch_shapes=[
            pltpu.SMEM(channel_shift.shape[::-1], jnp.int32),
            pltpu.SMEM(section_shift.shape, jnp.int32),
            pltpu.VMEM(filter_bank.shape, jnp.float32),
            pltpu.VMEM((GROUP, (TILES + 1) * chan_dev, LANES), jnp.float32),
            pltpu.VMEM((LANES * TILES, LANES), jnp.float32),
            pltpu.VMEM((filters * LANES, 6 * LANES), jnp.bfloat16),
            pltpu.VMEM((GROUP, filters, LANES), jnp.float32),
            dma((3,)),
            dma,
            dma((GROUP,)),
            dma((GROUP,)),
            dma,
            dma((GROUP,)),
            dma((GROUP,)),
            dma((GROUP,)),
        ],
        compiler_params=pltpu.CompilerParams(
            collective_id=0, has_side_effects=True, vmem_limit_bytes=60 * 2**20
        ),
    )(channel_shift.T, section_shift, filter_bank, by_tile)
    return maps.transpose(2, 0, 1)


def fits_fused(mesh, intensity, channel_shift, section_shift, filter_bank):
    groups, halves = mesh.shape["freq"], mesh.shape["tm"]
    samples = intensity.shape[1] // halves
    channels, trials_each = channel_shift.shape
    own = samples // groups
    reach = CHAN_MAX + SHIFT_UNIT * (2 ** section_shift.shape[0] - 1) + LANES
    return (
        groups == GROUP
        and halves == 2
        and channels == 8 * GROUP
        and trials_each == 2
        and filter_bank.shape == (8, LANES)
        and own % (2 * LANES) == 0
        and BLOCK % own == 0
        and reach <= own
        and own + reach <= (TILES - 1) * LANES
    )


def solution(mesh):
    in_specs = (P(("beam", "freq"), "tm"), P(), P(), P())
    out_specs = P(("beam", "freq"), None, "tm")

    def whole(*arrays):
        chosen = fused_body if fits_fused(mesh, *arrays) else body
        return jax.shard_map(
            chosen, mesh=mesh, in_specs=in_specs, out_specs=out_specs, check_vma=False
        )(*arrays)

    return whole
```
